32 devices in a mesh: ex: 8 (over z, x), ey: 4 (over y, core).
Axes of the slice: x: 2, y: 2, z: 4, core: 2. Of those that a mesh axis runs over, the one named last changes fastest.
Arguments:
- weights: bfloat16 [32, 7168, 1536], P(('ex', 'ey')), may hold values from -6 to 6
- fisher: float32 [32, 7168], P(('ex', 'ey')), may hold values from 0.3 to 3
- start: bfloat16 [7168, 128], P(('ex', 'ey')), may hold values from -6 to 6
Outputs:
- basis: float32 [7168, 128], P(('ex', 'ey'))
- coeffs: bfloat16 [32, 128, 1536], P(('ex', 'ey'))
The draws below stay inside these ranges and needn't reach their ends.
All inputs are finite; a program needn't handle non-finite values.
Results may differ from the reference program's by a relative error of at most 0.0054.
Values may be sent and summed in bfloat16 or wider, within the bound.
A program may use at most 128 MiB of HBM per device.

```python
import math
import jax
import jax.numpy as jnp
from jax import lax

D = 7168
FF = 1536
RANK = 128
EXPERTS = 32


def levels(stream_key, shape, pieces, smallest, high):
    def one(dim, blocks):
        draws = jax.random.uniform(jax.random.fold_in(jax.random.fold_in(stream_key, 6), dim), (blocks,), jnp.float32, smallest / len(pieces), high / len(pieces))
        return jnp.repeat(jnp.exp(draws), shape[dim] // blocks).reshape((-1,) + (1,) * (len(shape) - dim - 1))

    factor_of = one(*pieces[0])
    for cut in pieces[1:]:
        factor_of = factor_of * one(*cut)
    return factor_of


def centred(own_key, shape, scale, most, split=(), dtype=jnp.bfloat16):
    array = jax.random.normal(own_key, shape, jnp.float32) * scale
    if len(split) > 0:
        array = levels(own_key, shape, split, -0.22, 0.18) * array
    return jnp.clip(array, min=-most, max=most).astype(dtype)


def setup_inputs(seed: int = 0) -> dict:
    seeds = jax.random.split(jax.random.key(seed), 4)
    return {
        "weights": centred(seeds[0], (EXPERTS, D, FF), 1.0, 6.0, ((0, 32),)),
        "fisher": jnp.clip(jnp.exp(math.log(3.0) - 2.3025851 * jax.random.uniform(seeds[1], (EXPERTS, D), jnp.float32) ** levels(seeds[1], (EXPERTS, D), ((0, 32),), -0.2, 0.2)), 0.3, 3.0),
        "start": centred(seeds[2], (D, RANK), 1.0, 6.0, ((0, 32),)),
    }


def reference(weights, fisher, start):
    start_f = start.astype(jnp.float32)

    def add_expert(total, items):
        matrix, row_weight = items
        weighted = (row_weight[:, None] * start_f).astype(jnp.bfloat16)
        projected = jnp.dot(matrix.T.astype(jnp.float32), weighted.astype(jnp.float32), preferred_element_type=jnp.float32).astype(jnp.bfloat16)
        term = jnp.dot(matrix.astype(jnp.float32), projected.astype(jnp.float32), preferred_element_type=jnp.float32) * row_weight[:, None]
        return (total + term, None)
    sketch, unused = lax.scan(add_expert, jnp.zeros((D, RANK), jnp.float32), (weights, fisher))
    gram = jnp.dot(sketch.T, sketch, precision=lax.Precision.HIGHEST)
    lower = jnp.linalg.cholesky(gram)
    ortho = lax.linalg.triangular_solve(lower, sketch, left_side=False, lower=True, transpose_a=True)
    basis = ortho * jnp.sqrt(jnp.float32(D))

    def project(items):
        matrix, row_weight = items
        scaled = (row_weight[:, None] * ortho).astype(jnp.bfloat16)
        return jnp.dot(scaled.T.astype(jnp.float32), matrix.astype(jnp.float32), preferred_element_type=jnp.float32).astype(jnp.bfloat16)
    coeffs = lax.map(project, (weights, fisher))
    return (basis, coeffs)
```

```python
import functools
import math

import jax
import jax.numpy as jnp
from jax import lax
from jax.experimental import pallas as pl
from jax.experimental.pallas import tpu as pltpu
from jax.sharding import PartitionSpec as P

MESH = pl.DeviceIdType.MESH
BF16 = jnp.bfloat16
F32 = jnp.float32
HIGHEST = lax.Precision.HIGHEST
PANEL = 16


def power_kernel(
    Z,
    w_hbm, fisher_ref, start_ref,
    sketch_ref, gram_ref, raw_ref,
    w, fcol, starts, sketches, term, proj,
    core_out, core_in, one_out, one_in, two_out, two_in, z_out, z_in,
    w_sem, send_sem, recv_sem,
):
    ex, ey = lax.axis_index("ex"), lax.axis_index("ey")
    z, x, y, c = ex // 2, ex % 2, ey // 2, ey % 2
    rows, rank = start_ref.shape
    half = rows // 2
    chunk = 8 * rows
    width = w.shape[1]

    def z_of(k):
        low = (z % 2 + k % 2) % 2
        high = (z // 2 + k // 2) % 2
        return high * 2 + low

    z_peer = {k: (z_of(k) * 2 + x, ey) for k in range(1, Z)}
    x_peer = (z * 2 + (1 - x), ey)
    y_peer = (ex, (1 - y) * 2 + c)
    c_peer = (ex, y * 2 + (1 - c))

    def w_copy(k):
        at = pl.ds(pl.multiple_of(z_of(k) * chunk, chunk), chunk)
        return pltpu.make_async_copy(w_hbm.at[at], w.at[at], w_sem.at[k])

    for k in range(Z):
        w_copy(k).start()

    barrier = pltpu.get_barrier_semaphore()
    peers = [*z_peer.values(), x_peer, y_peer, c_peer]
    for peer in peers:
        pl.semaphore_signal(barrier, inc=1, device_id=peer, device_id_type=MESH)
    starts[z, x, y, c] = start_ref[...]
    pl.semaphore_wait(barrier, len(peers))

    copies = {}

    def send(key, src, dst, peer):
        i = len(copies)
        copies[key] = pltpu.make_async_remote_copy(
            src_ref=src, dst_ref=dst, send_sem=send_sem.at[i], recv_sem=recv_sem.at[i],
            device_id=peer, device_id_type=MESH,
        )
        copies[key].start()

    low, high = pl.ds(0, half), pl.ds(half, half)

    def gather(name, buf, ready, work=None):
        for k in range(1, Z):
            send((name, "z", k), buf.at[z, x, y, c], buf.at[z, x, y, c], z_peer[k])

        def first(k):
            if k > 0:
                copies[name, "z", k].wait_recv()
            a, b = buf.at[z_of(k), x, y, c, low], buf.at[z_of(k), x, y, c, high]
            send((name, 1, 0, k), a, a, x_peer)
            send((name, 1, 1, k), b, b, y_peer)

        def second(k):
            copies[name, 1, 0, k].wait_recv()
            a = buf.at[z_of(k), :, y, c, low]
            send((name, 2, 0, k), a, a, y_peer)
            copies[name, 1, 1, k].wait_recv()
            b = buf.at[z_of(k), x, :, c, high]
            send((name, 2, 1, k), b, b, x_peer)

        def third(k):
            copies[name, 2, 0, k].wait_recv()
            copies[name, 2, 1, k].wait_recv()
            a = buf.at[z_of(k), :, :, c]
            send((name, 3, k), a, a, c_peer)

        def fourth(k):
            copies[name, 3, k].wait_recv()
            ready(k)

        for t in range(Z + 3):
            for stage, f in enumerate((first, second, third)):
                if 0 <= t - stage < Z:
                    f(t - stage)
            if work is not None and t == 0:
                work()
            if 0 <= t - 3 < Z:
                fourth(t - 3)

    def w_rows(k):
        return w.at[pl.ds(pl.multiple_of(z_of(k) * chunk, chunk), chunk)]

    def turned(buf, k):
        return buf[z_of(k)].reshape(chunk, rank).astype(F32).T

    def add_product(out, left, k):
        matrix = w_rows(k)
        tile = 512
        for n in range(width // tile):
            at = slice(n * tile, (n + 1) * tile)
            part = jnp.dot(left, matrix[:, at], preferred_element_type=F32)
            out[:, at] = part if k == 0 else out[:, at] + part

    def columns():
        for q in range(Z):
            fcol[q] = jnp.broadcast_to(fisher_ref[q], (rank, chunk)).T

    def project(k):
        left = (turned(starts, k) * fisher_ref[z_of(k)]).astype(BF16)
        w_copy(k).wait()
        add_product(raw_ref, left, k)

    gather("start", starts, project, columns)
    proj[...] = raw_ref[...].T.astype(BF16)

    def compute(k):
        q = z_of(k)

        def pair(i, carry):
            at = pl.ds(pl.multiple_of(q * chunk + i * 2 * rows, 2 * rows), 2 * rows)
            part = jnp.dot(w[at], proj[...], preferred_element_type=F32)
            inner = pl.ds(pl.multiple_of(i * 2 * rows, 2 * rows), 2 * rows)
            part = part * fcol[q, inner]
            term[q, i // 2, i % 2] = part.reshape(2, rows, rank)
            core_out[k, i // 2, i % 2] = term[q, i // 2, i % 2, 1 - c].astype(BF16)
            return carry

        lax.fori_loop(0, 4, pair, 0)
        send(("sum", 0, k), core_out.at[k], core_in.at[k], c_peer)

    def sum_core(k):
        q = z_of(k)
        copies["sum", 0, k].wait_recv()
        for i in range(2):
            for j in range(2):
                term[q, i, j, c] = term[q, i, j, c] + core_in[k, i, j].astype(F32)
        for i in range(2):
            one_out[0, k, i] = term[q, i, 1 - y, c, low].astype(BF16)
            one_out[1, k, i] = term[q, 1 - x, i, c, high].astype(BF16)
        send(("sum", 1, 0, k), one_out.at[0, k], one_in.at[0, k], y_peer)
        send(("sum", 1, 1, k), one_out.at[1, k], one_in.at[1, k], x_peer)

    def sum_one(k):
        q = z_of(k)
        copies["sum", 1, 0, k].wait_recv()
        two_out[0, k] = (term[q, 1 - x, y, c, low] + one_in[0, k, 1 - x].astype(F32)).astype(BF16)
        send(("sum", 2, 0, k), two_out.at[0, k], two_in.at[0, k], x_peer)
        copies["sum", 1, 1, k].wait_recv()
        two_out[1, k] = (term[q, x, 1 - y, c, high] + one_in[1, k, 1 - y].astype(F32)).astype(BF16)
        send(("sum", 2, 1, k), two_out.at[1, k], two_in.at[1, k], y_peer)

    def sum_two(k):
        q = z_of(k)
        copies["sum", 2, 0, k].wait_recv()
        copies["sum", 2, 1, k].wait_recv()
        top = term[q, x, y, c, low] + one_in[0, k, x].astype(F32) + two_in[0, k].astype(F32)
        bottom = term[q, x, y, c, high] + one_in[1, k, y].astype(F32) + two_in[1, k].astype(F32)
        if k > 0:
            z_out[k, low] = top.astype(BF16)
            z_out[k, high] = bottom.astype(BF16)
            send(("sum", 3, k), z_out.at[k], z_in.at[k], z_peer[k])
        else:
            sketch_ref[low] = top
            sketch_ref[high] = bottom

    order = list(range(Z))[::-1]
    for t in range(Z + 3):
        for stage, f in enumerate((compute, sum_core, sum_one, sum_two)):
            if 0 <= t - stage < Z:
                f(order[t - stage])
    total = sketch_ref[...]
    for k in order[:-1]:
        copies["sum", 3, k].wait_recv()
        total = total + z_in[k].astype(F32)
    sketch_ref[...] = total
    sketches[z, x, y, c] = total.astype(BF16)

    def finish(k):
        plain = turned(sketches, k)
        part = jnp.dot(
            plain.astype(BF16), sketches[z_of(k)].reshape(chunk, rank), preferred_element_type=F32
        )
        gram_ref[...] = part if k == 0 else gram_ref[...] + part
        add_product(raw_ref, (plain * fisher_ref[z_of(k)]).astype(BF16), k)

    gather("sketch", sketches, finish)
    for copy in copies.values():
        copy.wait_send()


def basis_kernel(scale, sketch_ref, gram_ref, raw_ref, basis_ref, coeffs_ref, work):
    n = gram_ref.shape[0]
    work[:, :n] = gram_ref[...]
    i0 = lax.broadcasted_iota(jnp.int32, (n, n), 0)
    i1 = lax.broadcasted_iota(jnp.int32, (n, n), 1)
    work[:, n:] = jnp.where(i0 == i1, 1.0, 0.0).astype(F32)
    line = lax.broadcasted_iota(jnp.int32, (PANEL, 1), 0)
    for p in range(n // PANEL):
        base = p * PANEL
        panel = work[base : base + PANEL, :]
        for j in range(PANEL):
            column = panel[:, base + j : base + j + 1]
            r = lax.rsqrt(panel[j : j + 1, base + j : base + j + 1])
            row = panel[j : j + 1, :] * r
            factor = jnp.where(line > j, column * r, 0.0)
            panel = jnp.where(line == j, row, panel - factor * row)
        work[base : base + PANEL, :] = panel
        end = base + PANEL
        if end < n:
            update = lax.dot_general(
                panel[:, :n], panel, (((0,), (0,)), ((), ())), precision=HIGHEST, preferred_element_type=F32
            )
            work[end:, :] = work[end:, :] - update[end:, :]
    inverse = work[:, n:]
    basis_ref[...] = scale * lax.dot_general(
        sketch_ref[...], inverse, (((1,), (1,)), ((), ())), precision=HIGHEST, preferred_element_type=F32
    )
    coeffs_ref[...] = jnp.dot(
        inverse, raw_ref[...], precision=HIGHEST, preferred_element_type=F32
    ).astype(BF16)


def fused_body(Z, weights, fisher, start):
    matrix = weights[0]
    depth, width = matrix.shape
    rows, rank = start.shape
    half, chunk = rows // 2, 8 * rows
    vmem = pl.BlockSpec(memory_space=pltpu.VMEM)
    n_copies = 3 * (Z - 1 + 5 * Z)
    sketch, gram, raw = pl.pallas_call(
        functools.partial(power_kernel, Z),
        out_shape=(
            jax.ShapeDtypeStruct((rows, rank), F32),
            jax.ShapeDtypeStruct((rank, rank), F32),
            jax.ShapeDtypeStruct((rank, width), F32),
        ),
        in_specs=[pl.BlockSpec(memory_space=pl.ANY), vmem, vmem],
        out_specs=(vmem, vmem, vmem),
        scratch_shapes=[
            pltpu.VMEM((depth, width), BF16),
            pltpu.VMEM((Z, chunk, rank), F32),
            pltpu.VMEM((Z, 2, 2, 2, rows, rank), BF16),
            pltpu.VMEM((Z, 2, 2, 2, rows, rank), BF16),
            pltpu.VMEM((Z, 2, 2, 2, rows, rank), F32),
            pltpu.VMEM((width, rank), BF16),
            pltpu.VMEM((Z, 2, 2, rows, rank), BF16),
            pltpu.VMEM((Z, 2, 2, rows, rank), BF16),
            pltpu.VMEM((2, Z, 2, half, rank), BF16),
            pltpu.VMEM((2, Z, 2, half, rank), BF16),
            pltpu.VMEM((2, Z, half, rank), BF16),
            pltpu.VMEM((2, Z, half, rank), BF16),
            pltpu.VMEM((Z, rows, rank), BF16),
            pltpu.VMEM((Z, rows, rank), BF16),
            pltpu.SemaphoreType.DMA((Z,)),
            pltpu.SemaphoreType.DMA((n_copies,)),
            pltpu.SemaphoreType.DMA((n_copies,)),
        ],
        compiler_params=pltpu.CompilerParams(
            collective_id=0, has_side_effects=True, vmem_limit_bytes=56 * 2**20
        ),
        cost_estimate=pl.CostEstimate(
            flops=6 * depth * width * rank, bytes_accessed=2 * depth * width, transcendentals=0
        ),
    )(matrix, fisher.reshape(Z, 1, chunk), start)
    basis, coeffs = pl.pallas_call(
        functools.partial(basis_kernel, math.sqrt(depth)),
        out_shape=(
            jax.ShapeDtypeStruct((rows, rank), F32),
            jax.ShapeDtypeStruct((rank, width), BF16),
        ),
        in_specs=[vmem, vmem, vmem],
        out_specs=(vmem, vmem),
        scratch_shapes=[pltpu.VMEM((rank, 2 * rank), F32)],
        compiler_params=pltpu.CompilerParams(vmem_limit_bytes=32 * 2**20),
    )(sketch, gram, raw)
    return basis, coeffs[None]


def plain_body(weights, fisher, start):
    axes = ("ex", "ey")
    matrix, scale = weights[0], fisher[0][:, None]
    width = matrix.shape[0]
    whole = lax.all_gather(start, axes, axis=0, tiled=True).astype(F32)
    projected = lax.dot_general(
        matrix, (scale * whole).astype(BF16), (((0,), (0,)), ((), ())), preferred_element_type=F32
    ).astype(BF16)
    term = jnp.dot(matrix, projected, preferred_element_type=F32) * scale
    sketch = lax.psum_scatter(term, axes, scatter_dimension=0, tiled=True)
    gram = lax.psum(jnp.dot(sketch.T, sketch, precision=HIGHEST), axes)
    lower = jnp.linalg.cholesky(gram)
    ortho = lax.linalg.triangular_solve(lower, sketch, left_side=False, lower=True, transpose_a=True)
    scaled = (scale * lax.all_gather(ortho, axes, axis=0, tiled=True)).astype(BF16)
    coeffs = lax.dot_general(scaled, matrix, (((0,), (0,)), ((), ())), preferred_element_type=F32)
    return ortho * jnp.sqrt(jnp.float32(width)), coeffs.astype(BF16)[None]


def solution(mesh):
    placed = (P(("ex", "ey"), None, None), P(("ex", "ey"), None), P(("ex", "ey"), None))
    if mesh.shape["ex"] == 8 and mesh.shape["ey"] == 4:
        body = functools.partial(fused_body, mesh.shape["ex"] // 2)
    else:
        body = plain_body
    return jax.shard_map(
        body,
        mesh=mesh,
        in_specs=placed,
        out_specs=(P(("ex", "ey"), None), P(("ex", "ey"), None, None)),
        check_vma=False,
    )
```

```python
import functools
import math

import jax
import jax.numpy as jnp
from jax import lax
from jax.experimental import pallas as pl
from jax.experimental.pallas import tpu as pltpu
from jax.sharding import PartitionSpec as P

MESH = pl.DeviceIdType.MESH
BF16 = jnp.bfloat16
F32 = jnp.float32
HIGHEST = lax.Precision.HIGHEST
PANEL = 16
GROUP = 4


def power_kernel(
    Z,
    w_hbm, fisher_ref, start_ref,
    basis_ref, coeffs_ref,
    sketch_ref, gram_ref, raw_ref, work,
    w, fcol, starts, sketches, term, proj,
    core_out, core_in, one_out, one_in, two_out, two_in, z_out, z_in,
    w_sem, send_sem, recv_sem,
):
    ex, ey = lax.axis_index("ex"), lax.axis_index("ey")
    z, x, y, c = ex // 2, ex % 2, ey // 2, ey % 2
    rows, rank = start_ref.shape
    half = rows // 2
    chunk = 8 * rows
    width = w.shape[1]

    def z_of(k):
        low = (z % 2 + k % 2) % 2
        high = (z // 2 + k // 2) % 2
        return high * 2 + low

    z_peer = {k: (z_of(k) * 2 + x, ey) for k in range(1, Z)}
    x_peer = (z * 2 + (1 - x), ey)
    y_peer = (ex, (1 - y) * 2 + c)
    c_peer = (ex, y * 2 + (1 - c))

    def w_copy(k):
        at = pl.ds(pl.multiple_of(z_of(k) * chunk, chunk), chunk)
        return pltpu.make_async_copy(w_hbm.at[at], w.at[at], w_sem.at[k])

    for k in range(Z):
        w_copy(k).start()

    barrier = pltpu.get_barrier_semaphore()
    peers = [*z_peer.values(), x_peer, y_peer, c_peer]
    for peer in peers:
        pl.semaphore_signal(barrier, inc=1, device_id=peer, device_id_type=MESH)
    starts[z, x, y, c] = start_ref[...]
    pl.semaphore_wait(barrier, len(peers))

    copies = {}

    def send(key, src, dst, peer):
        i = len(copies)
        copies[key] = pltpu.make_async_remote_copy(
            src_ref=src, dst_ref=dst, send_sem=send_sem.at[i], recv_sem=recv_sem.at[i],
            device_id=peer, device_id_type=MESH,
        )
        copies[key].start()

    low, high = pl.ds(0, half), pl.ds(half, half)

    def gather(name, buf, ready, work=None):
        for k in range(1, Z):
            send((name, "z", k), buf.at[z, x, y, c], buf.at[z, x, y, c], z_peer[k])

        def first(k):
            if k > 0:
                copies[name, "z", k].wait_recv()
            a, b = buf.at[z_of(k), x, y, c, low], buf.at[z_of(k), x, y, c, high]
            send((name, 1, 0, k), a, a, x_peer)
            send((name, 1, 1, k), b, b, y_peer)

        def second(k):
            copies[name, 1, 0, k].wait_recv()
            a = buf.at[z_of(k), :, y, c, low]
            send((name, 2, 0, k), a, a, y_peer)
            copies[name, 1, 1, k].wait_recv()
            b = buf.at[z_of(k), x, :, c, high]
            send((name, 2, 1, k), b, b, x_peer)

        def third(k):
            copies[name, 2, 0, k].wait_recv()
            copies[name, 2, 1, k].wait_recv()
            a = buf.at[z_of(k), :, :, c]
            send((name, 3, k), a, a, c_peer)

        def fourth(k):
            copies[name, 3, k].wait_recv()
            ready(k)

        for t in range(Z + 3):
            for stage, f in enumerate((first, second, third)):
                if 0 <= t - stage < Z:
                    f(t - stage)
            if work is not None and t == 0:
                work()
            if 0 <= t - 3 < Z:
                fourth(t - 3)

    def w_rows(k):
        return w.at[pl.ds(pl.multiple_of(z_of(k) * chunk, chunk), chunk)]

    def turned(buf, k):
        return buf[z_of(k)].reshape(chunk, rank).astype(F32).T

    def add_product(out, left, k):
        matrix = w_rows(k)
        tile = 512
        for n in range(width // tile):
            at = slice(n * tile, (n + 1) * tile)
            part = jnp.dot(left, matrix[:, at], preferred_element_type=F32)
            out[:, at] = part if k == 0 else out[:, at] + part

    def columns():
        for q in range(Z):
            fcol[q] = jnp.broadcast_to(fisher_ref[q], (rank, chunk)).T

    def project(k):
        left = (turned(starts, k) * fisher_ref[z_of(k)]).astype(BF16)
        w_copy(k).wait()
        add_product(raw_ref, left, k)

    gather("start", starts, project, columns)
    proj[...] = raw_ref[...].T.astype(BF16)

    def compute(k, between):
        q = z_of(k)

        def pair(i):
            at = pl.ds(pl.multiple_of(q * chunk + i * 2 * rows, 2 * rows), 2 * rows)
            part = jnp.dot(w[at], proj[...], preferred_element_type=F32)
            inner = pl.ds(i * 2 * rows, 2 * rows)
            part = part * fcol[q, inner]
            term[q, i // 2, i % 2] = part.reshape(2, rows, rank)
            core_out[k, i // 2, i % 2] = term[q, i // 2, i % 2, 1 - c].astype(BF16)

        for i in range(4):
            pair(i)
            if i < 3:
                between[i]()
        send(("sum", 0, k), core_out.at[k], core_in.at[k], c_peer)

    def sum_core(k):
        q = z_of(k)
        copies["sum", 0, k].wait_recv()
        for i in range(2):
            for j in range(2):
                term[q, i, j, c] = term[q, i, j, c] + core_in[k, i, j].astype(F32)
        for i in range(2):
            one_out[0, k, i] = term[q, i, 1 - y, c, low].astype(BF16)
            one_out[1, k, i] = term[q, 1 - x, i, c, high].astype(BF16)
        send(("sum", 1, 0, k), one_out.at[0, k], one_in.at[0, k], y_peer)
        send(("sum", 1, 1, k), one_out.at[1, k], one_in.at[1, k], x_peer)

    def sum_one(k):
        q = z_of(k)
        copies["sum", 1, 0, k].wait_recv()
        two_out[0, k] = (term[q, 1 - x, y, c, low] + one_in[0, k, 1 - x].astype(F32)).astype(BF16)
        send(("sum", 2, 0, k), two_out.at[0, k], two_in.at[0, k], x_peer)
        copies["sum", 1, 1, k].wait_recv()
        two_out[1, k] = (term[q, x, 1 - y, c, high] + one_in[1, k, 1 - y].astype(F32)).astype(BF16)
        send(("sum", 2, 1, k), two_out.at[1, k], two_in.at[1, k], y_peer)

    def sum_two(k):
        q = z_of(k)
        copies["sum", 2, 0, k].wait_recv()
        copies["sum", 2, 1, k].wait_recv()
        top = term[q, x, y, c, low] + one_in[0, k, x].astype(F32) + two_in[0, k].astype(F32)
        bottom = term[q, x, y, c, high] + one_in[1, k, y].astype(F32) + two_in[1, k].astype(F32)
        if k > 0:
            z_out[k, low] = top.astype(BF16)
            z_out[k, high] = bottom.astype(BF16)
            send(("sum", 3, k), z_out.at[k], z_in.at[k], z_peer[k])
        else:
            sketch_ref[low] = top
            sketch_ref[high] = bottom

    order = list(range(Z))[::-1]
    for t in range(Z + 3):
        between = [
            functools.partial(f, order[t - stage]) if 0 <= t - stage < Z else lambda: None
            for stage, f in enumerate((sum_core, sum_one, sum_two), 1)
        ]
        if t < Z:
            compute(order[t], between)
        else:
            for f in between:
                f()
    total = sketch_ref[...]
    for k in order[:-1]:
        copies["sum", 3, k].wait_recv()
        total = total + z_in[k].astype(F32)
    sketch_ref[...] = total
    sketches[z, x, y, c] = total.astype(BF16)

    def finish(k):
        plain = turned(sketches, k)
        part = jnp.dot(
            plain.astype(BF16), sketches[z_of(k)].reshape(chunk, rank), preferred_element_type=F32
        )
        gram_ref[...] = part if k == 0 else gram_ref[...] + part
        add_product(raw_ref, (plain * fisher_ref[z_of(k)]).astype(BF16), k)

    gather("sketch", sketches, finish)
    finish_basis(math.sqrt(Z * chunk), sketch_ref, gram_ref, raw_ref, basis_ref, coeffs_ref, work)
    for copy in copies.values():
        copy.wait_send()


def finish_basis(scale, sketch_ref, gram_ref, raw_ref, basis_ref, coeffs_ref, work):
    n = gram_ref.shape[0]
    work[:, :n] = gram_ref[...]
    i0 = lax.broadcasted_iota(jnp.int32, (n, n), 0)
    i1 = lax.broadcasted_iota(jnp.int32, (n, n), 1)
    work[:, n:] = jnp.where(i0 == i1, 1.0, 0.0).astype(F32)
    line = lax.broadcasted_iota(jnp.int32, (PANEL, n), 0)

    def spread(a):
        return jnp.broadcast_to(a, (PANEL, n))

    for p in range(n // PANEL):
        base = p * PANEL
        left, right = work[base : base + PANEL, :n], work[base : base + PANEL, n:]
        for j in range(0, PANEL, GROUP):
            group = range(GROUP)
            lrow = [spread(left[j + i : j + i + 1, :]) for i in group]
            rrow = [spread(right[j + i : j + i + 1, :]) for i in group]
            column = [spread(left[:, base + j + i : base + j + i + 1]) for i in group]
            corner = {
                (i, m): spread(left[j + i : j + i + 1, base + j + m : base + j + m + 1])
                for i in group for m in group if m >= i
            }
            for i in group:
                r = lax.rsqrt(corner[i, i])
                lrow[i], rrow[i], column[i] = lrow[i] * r, rrow[i] * r, column[i] * r
                for m in range(i + 1, GROUP):
                    corner[i, m] = corner[i, m] * r
                for m in range(i + 1, GROUP):
                    f = corner[i, m]
                    lrow[m], rrow[m] = lrow[m] - f * lrow[i], rrow[m] - f * rrow[i]
                    column[m] = column[m] - f * column[i]
                    for q in range(m, GROUP):
                        corner[m, q] = corner[m, q] - f * corner[i, q]
            for i in group:
                f = jnp.where(line >= j + GROUP, column[i], 0.0)
                left = jnp.where(line == j + i, lrow[i], left - f * lrow[i])
                right = jnp.where(line == j + i, rrow[i], right - f * rrow[i])
        panel = jnp.concatenate([left, right], axis=1)
        work[base : base + PANEL, :] = panel
        end = base + PANEL
        if end < n:
            update = lax.dot_general(
                panel[:, :n], panel, (((0,), (0,)), ((), ())), precision=HIGHEST, preferred_element_type=F32
            )
            work[end:, :] = work[end:, :] - update[end:, :]
    inverse = work[:, n:]
    basis_ref[...] = scale * lax.dot_general(
        sketch_ref[...], inverse, (((1,), (1,)), ((), ())), precision=HIGHEST, preferred_element_type=F32
    )
    coeffs_ref[...] = jnp.dot(
        inverse, raw_ref[...], precision=HIGHEST, preferred_element_type=F32
    ).astype(BF16)


def fused_body(Z, weights, fisher, start):
    matrix = weights[0]
    depth, width = matrix.shape
    rows, rank = start.shape
    half, chunk = rows // 2, 8 * rows
    vmem = pl.BlockSpec(memory_space=pltpu.VMEM)
    n_copies = 3 * (Z - 1 + 5 * Z)
    basis, coeffs = pl.pallas_call(
        functools.partial(power_kernel, Z),
        out_shape=(
            jax.ShapeDtypeStruct((rows, rank), F32),
            jax.ShapeDtypeStruct((rank, width), BF16),
        ),
        in_specs=[pl.BlockSpec(memory_space=pl.ANY), vmem, vmem],
        out_specs=(vmem, vmem),
        scratch_shapes=[
            pltpu.VMEM((rows, rank), F32),
            pltpu.VMEM((rank, rank), F32),
            pltpu.VMEM((rank, width), F32),
            pltpu.VMEM((rank, 2 * rank), F32),
            pltpu.VMEM((depth, width), BF16),
            pltpu.VMEM((Z, chunk, rank), F32),
            pltpu.VMEM((Z, 2, 2, 2, rows, rank), BF16),
            pltpu.VMEM((Z, 2, 2, 2, rows, rank), BF16),
            pltpu.VMEM((Z, 2, 2, 2, rows, rank), F32),
            pltpu.VMEM((width, rank), BF16),
            pltpu.VMEM((Z, 2, 2, rows, rank), BF16),
            pltpu.VMEM((Z, 2, 2, rows, rank), BF16),
            pltpu.VMEM((2, Z, 2, half, rank), BF16),
            pltpu.VMEM((2, Z, 2, half, rank), BF16),
            pltpu.VMEM((2, Z, half, rank), BF16),
            pltpu.VMEM((2, Z, half, rank), BF16),
            pltpu.VMEM((Z, rows, rank), BF16),
            pltpu.VMEM((Z, rows, rank), BF16),
            pltpu.SemaphoreType.DMA((Z,)),
            pltpu.SemaphoreType.DMA((n_copies,)),
            pltpu.SemaphoreType.DMA((n_copies,)),
        ],
        compiler_params=pltpu.CompilerParams(
            collective_id=0, has_side_effects=True, vmem_limit_bytes=56 * 2**20
        ),
        cost_estimate=pl.CostEstimate(
            flops=6 * depth * width * rank, bytes_accessed=2 * depth * width, transcendentals=0
        ),
    )(matrix, fisher.reshape(Z, 1, chunk), start)
    return basis, coeffs[None]


def plain_body(weights, fisher, start):
    axes = ("ex", "ey")
    matrix, scale = weights[0], fisher[0][:, None]
    width = matrix.shape[0]
    whole = lax.all_gather(start, axes, axis=0, tiled=True).astype(F32)
    projected = lax.dot_general(
        matrix, (scale * whole).astype(BF16), (((0,), (0,)), ((), ())), preferred_element_type=F32
    ).astype(BF16)
    term = jnp.dot(matrix, projected, preferred_element_type=F32) * scale
    sketch = lax.psum_scatter(term, axes, scatter_dimension=0, tiled=True)
    gram = lax.psum(jnp.dot(sketch.T, sketch, precision=HIGHEST), axes)
    lower = jnp.linalg.cholesky(gram)
    ortho = lax.linalg.triangular_solve(lower, sketch, left_side=False, lower=True, transpose_a=True)
    scaled = (scale * lax.all_gather(ortho, axes, axis=0, tiled=True)).astype(BF16)
    coeffs = lax.dot_general(scaled, matrix, (((0,), (0,)), ((), ())), preferred_element_type=F32)
    return ortho * jnp.sqrt(jnp.float32(width)), coeffs.astype(BF16)[None]


def solution(mesh):
    placed = (P(("ex", "ey"), None, None), P(("ex", "ey"), None), P(("ex", "ey"), None))
    if mesh.shape["ex"] == 8 and mesh.shape["ey"] == 4:
        body = functools.partial(fused_body, mesh.shape["ex"] // 2)
    else:
        body = plain_body
    return jax.shard_map(
        body,
        mesh=mesh,
        in_specs=placed,
        out_specs=(P(("ex", "ey"), None), P(("ex", "ey"), None, None)),
        check_vma=False,
    )
```
